32 devices in a mesh: grp: 2 (over x), gy: 16 (over z, y, core).
Axes of the slice: x: 2, y: 2, z: 4, core: 2. Of those that a mesh axis runs over, the one named last changes fastest.
Arguments:
- initial: float32 [64, 32, 256], P('gy', 'grp'), parts along dimension 1, may hold values from -1.2 to 1.2
Outputs:
- slab_ends: float32 [4, 64, 32, 256], P(None, 'gy', 'grp'), parts along dimension 2
The draws below stay inside these ranges and needn't reach their ends.
There are 2 independent parts, one for each index of `grp`. The reference program is written for one: setup_inputs(seed, part) draws one part's arguments, and reference() takes and returns one part's arrays. A program takes and returns all parts, laid end to end along the dimension named above; each array names one. Nothing has to cross between parts.
All inputs are finite; a program needn't handle non-finite values.
Results may differ from the reference program's by a relative error of at most 0.00002.
Values sent between devices are 32-bit elements; how exact they have to be, the bound alone decides.
A program may use at most 128 MiB of HBM per device.

```python
from functools import partial
import jax
import jax.numpy as jnp

NX = 16
NZ = 256
SLABS = 4
NY = 64


def draw_initial(key, part):
    key = jax.random.fold_in(key, 11)
    uniform_noise = jax.random.uniform(key, (NY, NX, NZ), jnp.float32, -1.0, 1.0)
    return uniform_noise


def setup_inputs(seed: int = 0, part: int = 0) -> dict:
    key_of = jax.random.split(jax.random.key(seed), 2)
    part_splits = jax.random.split(jax.random.fold_in(key_of[1], part), 2)
    return {
        "initial": draw_initial(jax.random.fold_in(jax.random.fold_in(key_of[1], part), 71), part),
    }


left_weights = (5.0 / 24.0, 1.0 / 3.0, -1.0 / 24.0)
right_weights = (-1.0 / 24.0, 1.0 / 3.0, 5.0 / 24.0)
slab_time = 0.25
half_step = 0.125
fine_coefficient = 1.0
coarse_coefficient = 0.25


def tendency(field, coefficient):
    beside = jnp.roll(field, -1, -3) + jnp.roll(field, 1, -3)
    beside = beside + jnp.roll(field, 1, -2) + jnp.roll(field, -1, -2)
    beside = beside + jnp.roll(field, 1, -1) + jnp.roll(field, -1, -1)
    return coefficient * (beside - 6.0 * field) + (field - field * field * field)


def quadrature(weights_row, first_term, middle_term, last_term):
    return slab_time * (weights_row[0] * first_term + weights_row[1] * middle_term + weights_row[2] * last_term)


def advance(node_value, new_tendency, old_tendency, forcing):
    return node_value + (half_step * (new_tendency - old_tendency) + forcing)


def restrict(field):
    sizes_now = field.shape
    blocks = field.reshape(sizes_now[:-3] + (sizes_now[-3] // 2, 2, sizes_now[-2] // 2, 2, sizes_now[-1] // 2, 2))
    return jnp.mean(blocks, axis=(-5, -3, -1))


def alternate(even_rows, odd_rows, along):
    paired = jnp.stack([even_rows, odd_rows], axis=along)
    new_shape = list(even_rows.shape)
    new_shape[along] = 2 * new_shape[along]
    return paired.reshape(new_shape)


def stretch(coarse, along):
    even_rows = 0.75 * coarse + 0.25 * jnp.roll(coarse, 1, along)
    odd_rows = 0.75 * coarse + 0.25 * jnp.roll(coarse, -1, along)
    return alternate(even_rows, odd_rows, along)


def prolong(coarse):
    return stretch(stretch(stretch(coarse, -3), -2), -1)


def spread_terms(start_tendency):
    rest_zero = quadrature(left_weights, start_tendency, start_tendency, start_tendency)
    rest_one = quadrature(right_weights, start_tendency, start_tendency, start_tendency)
    return start_tendency, rest_zero, start_tendency, rest_one


def stored_terms(forcing_slab, start_tendency):
    return forcing_slab[0], forcing_slab[1], forcing_slab[2], forcing_slab[3]


def build_forcing(coarse_tendency, mismatch):
    rest_zero = quadrature(left_weights, coarse_tendency[:, 0], coarse_tendency[:, 1], coarse_tendency[:, 2]) + quadrature(left_weights, mismatch[:, 0], mismatch[:, 1], mismatch[:, 2])
    rest_one = quadrature(right_weights, coarse_tendency[:, 0], coarse_tendency[:, 1], coarse_tendency[:, 2]) + quadrature(right_weights, mismatch[:, 0], mismatch[:, 1], mismatch[:, 2])
    return jnp.stack([coarse_tendency[:, 0], rest_zero, coarse_tendency[:, 1], rest_one], 1)


def coarse_slab(start_value, slab_terms):
    start_tendency = tendency(start_value, coarse_coefficient)
    fold_zero, rest_zero, fold_one, rest_one = slab_terms(start_tendency)
    node_one = advance(start_value, start_tendency, fold_zero, rest_zero)
    node_two = advance(node_one, tendency(node_one, coarse_coefficient), fold_one, rest_one)
    return node_one, node_two


def reference(initial):
    first_coarse = restrict(initial)
    start_value = first_coarse
    node_list = []
    for slab_index in range(SLABS):
        node_one, node_two = coarse_slab(start_value, spread_terms)
        node_list.append(jnp.stack([start_value, node_one, node_two]))
        start_value = node_two
    old_iterate = prolong(jnp.stack(node_list)).at[0, 0].set(initial)
    old_tendency = tendency(old_iterate, fine_coefficient)
    tend_zero = old_tendency[:, 0]
    tend_one = old_tendency[:, 1]
    tend_two = old_tendency[:, 2]
    new_one = advance(old_iterate[:, 0], tend_zero, tend_zero, quadrature(left_weights, tend_zero, tend_one, tend_two))
    new_tend_one = tendency(new_one, fine_coefficient)
    new_two = advance(new_one, new_tend_one, tend_one, quadrature(right_weights, tend_zero, tend_one, tend_two))
    new_tend_two = tendency(new_two, fine_coefficient)
    coarse_old = restrict(jnp.stack([old_iterate[:, 0], new_one, new_two], 1))
    coarse_tendency = tendency(coarse_old, coarse_coefficient)
    fine_average = restrict(jnp.stack([tend_zero, new_tend_one, new_tend_two], 1))
    forcing = build_forcing(coarse_tendency, fine_average - coarse_tendency)
    start_value = first_coarse
    difference_list = []
    for slab_index in range(SLABS):
        node_one, node_two = coarse_slab(start_value, partial(stored_terms, forcing[slab_index]))
        difference_list.append(node_two - coarse_old[slab_index, 2])
        start_value = node_two
    return new_two + prolong(jnp.stack(difference_list))
```

```python
import jax
import jax.numpy as jnp
from jax import lax
from jax.experimental import pallas as pl
from jax.experimental.pallas import tpu as pltpu
from jax.sharding import PartitionSpec as P

SLABS = 4
slab_time = 0.25
half_step = 0.125
left_weights = (5.0 / 24.0, 1.0 / 3.0, -1.0 / 24.0)
right_weights = (-1.0 / 24.0, 1.0 / 3.0, 5.0 / 24.0)
Q0 = tuple(slab_time * w for w in left_weights)
Q1 = tuple(slab_time * w for w in right_weights)

REACH = 5
OWN = 2
PARITIES = ((0, 0), (0, 1), (1, 0), (1, 1))


def lanes(x, shift):
    return pltpu.roll(x, shift % x.shape[-1], x.ndim - 1)


def rows(x, shift):
    return pltpu.roll(x, shift % x.shape[-2], x.ndim - 2)


def coarse_step(v):
    c = v[1:-1]
    beside = (v[2:] + v[:-2]) + (rows(c, 1) + rows(c, -1)) + (lanes(c, 1) + lanes(c, -1))
    return 0.03125 * beside + c * (0.9375 - 0.125 * (c * c))


def coarse_tendency(v):
    c = v[1:-1]
    beside = (v[2:] + v[:-2]) + (rows(c, 1) + rows(c, -1)) + (lanes(c, 1) + lanes(c, -1))
    return 0.25 * beside - c * (0.5 + c * c)


def fine_tendency(v):
    c = [p[1:-1] for p in v]
    out = []
    for k, (px, pz) in enumerate(PARITIES):
        x = c[2 * (1 - px) + pz]
        z = c[2 * px + 1 - pz]
        beside = (v[k][2:] + v[k][:-2]) + (x + rows(x, -1 if px else 1)) + (z + lanes(z, -1 if pz else 1))
        out.append(beside - c[k] * (5.0 + c[k] * c[k]))
    return out


def prolong(c):
    c = c * (1.0 / 64.0)
    triple = 3.0 * c
    out = []
    by_z = (triple + lanes(c, 1), triple + lanes(c, -1))
    planes = {}
    for pz in (0, 1):
        w = by_z[pz]
        triple = 3.0 * w
        planes[0, pz] = triple + rows(w, 1)
        planes[1, pz] = triple + rows(w, -1)
    for k in PARITIES:
        p = planes[k]
        triple = 3.0 * p
        odd = triple[:-1] + p[1:]
        even = triple[1:] + p[:-1]
        out.append(jnp.stack([odd, even], 1).reshape((2 * odd.shape[0],) + odd.shape[1:]))
    return out


def restrict(v):
    s = (v[0] + v[1]) + (v[2] + v[3])
    s = s.reshape((s.shape[0] // 2, 2) + s.shape[1:])
    return 0.125 * (s[:, 0] + s[:, 1])


def pick(x, table):
    high = x.astype(jnp.bfloat16)
    rest = x - high.astype(jnp.float32)
    middle = rest.astype(jnp.bfloat16)
    low = (rest - middle.astype(jnp.float32)).astype(jnp.bfloat16)
    dot = lambda p: jnp.dot(p, table, preferred_element_type=jnp.float32)
    return (dot(high) + dot(middle)) + dot(low)


def kernel(count, init_ref, out_ref, raw, fine, coarse, force0, force1, force2, force3, ends, new, stage, obuf,
           in_sem, out_sem, send_sem, recv_sem):
    me = lax.axis_index("gy")
    force = (force0, force1, force2, force3)

    def device(offset):
        return {"gy": lax.rem(me + (offset + count), count)}

    fetch = pltpu.make_async_copy(init_ref, raw, in_sem)
    fetch.start()
    barrier = pltpu.get_barrier_semaphore()
    for d in range(1, REACH + 1):
        for offset in (d, -d):
            pl.semaphore_signal(barrier, inc=1, device_id=device(offset))

    copies = []

    def send(src, dst, offset):
        k = len(copies)
        copy = pltpu.make_async_remote_copy(
            src_ref=src, dst_ref=dst, send_sem=send_sem.at[k], recv_sem=recv_sem.at[k], device_id=device(offset))
        copy.start()
        copies.append(copy)
        return copy

    a = lax.broadcasted_iota(jnp.int32, (256, 256), 0)
    b = lax.broadcasted_iota(jnp.int32, (256, 256), 1)
    part = (a == 2 * lax.rem(b, 128) + lax.div(b, 128)).astype(jnp.float32).astype(jnp.bfloat16)
    join = (b == 2 * lax.rem(a, 128) + lax.div(a, 128)).astype(jnp.float32).astype(jnp.bfloat16)

    fetch.wait()
    y = pick(raw[...].reshape(64, 256), part)
    stage[0, 0] = y[:, :128]
    stage[0, 1] = y[:, 128:]
    own = [stage[0, pz, pl.ds(px, 32, 2)].reshape(4, 8, 128) for px, pz in PARITIES]
    coarse[pl.ds(2 * REACH, OWN)] = restrict(own)
    for k in range(4):
        fine[pl.ds(3, 4), k] = own[k]

    pl.semaphore_wait(barrier, 2 * REACH)
    first_sends = []
    for d in range(REACH, 0, -1):
        for offset in (d, -d):
            first_sends.append(send(coarse.at[pl.ds(2 * REACH, OWN)],
                                    coarse.at[pl.ds(2 * REACH - 2 * offset, OWN)], offset))
    fine_sends = [send(fine.at[pl.ds(4, 3)], fine.at[pl.ds(0, 3)], 1),
                  send(fine.at[pl.ds(3, 3)], fine.at[pl.ds(7, 3)], -1)]

    for copy in first_sends:
        copy.wait_recv()
    s = coarse[...]
    nodes = [s[8:14]]
    for k in range(1, 9):
        s = coarse_step(s)
        nodes.append(s[8 - k:14 - k])

    for copy in fine_sends:
        copy.wait_recv()
    force_sends = []
    for n in range(SLABS):
        if n == 0:
            old0 = [fine[:, k] for k in range(4)]
        else:
            old0 = prolong(nodes[2 * n])
        old1 = prolong(nodes[2 * n + 1])
        old2 = prolong(nodes[2 * n + 2])
        f0 = fine_tendency(old0)
        f1 = fine_tendency(old1)
        f2 = fine_tendency(old2)
        one = [o[1:-1] + ((Q0[0] * x + Q0[1] * y) + Q0[2] * z) for o, x, y, z in zip(old0, f0, f1, f2)]
        g1 = fine_tendency(one)
        two = [o[1:-1] + (half_step * g + ((Q1[0] * x[1:-1] + (Q1[1] - half_step) * y[1:-1]) + Q1[2] * z[1:-1]))
               for o, g, x, y, z in zip(one, g1, f0, f1, f2)]
        g2 = fine_tendency(two)
        for k in range(4):
            new[n, k] = two[k][1:5]
        ends[pl.ds(1, 2), n] = restrict([t[1:5] for t in two])
        r0 = restrict([x[2:6] for x in f0])
        r1 = restrict([x[1:5] for x in g1])
        r2 = restrict(g2)
        c0 = coarse_tendency(restrict([o[1:9] for o in old0]))
        c1 = coarse_tendency(restrict(one))
        reach = 8 - 2 * n
        force[n][pl.ds(reach, OWN), 0] = (Q0[0] * r0 + Q0[1] * r1 + Q0[2] * r2) - half_step * c0
        force[n][pl.ds(reach, OWN), 1] = (Q1[0] * r0 + Q1[1] * r1 + Q1[2] * r2) - half_step * c1
        group = []
        for d in range(reach // 2, 0, -1):
            for offset in (d, -d):
                group.append(send(force[n].at[pl.ds(reach, OWN)],
                                  force[n].at[pl.ds(reach - 2 * offset, OWN)], offset))
        force_sends.append(group)
    end_sends = [send(ends.at[2], ends.at[0], 1), send(ends.at[1], ends.at[3], -1)]

    t = coarse[1:21]
    stores = []
    for n in range(SLABS):
        for copy in force_sends[n]:
            copy.wait_recv()
        t = coarse_step(t) + force[n][:, 0]
        reach = 8 - 2 * n
        t = coarse_step(t) + force[n][pl.ds(1, 2 * reach), 1]
        if n == 0:
            for copy in end_sends:
                copy.wait_recv()
        first = 8 - (2 * n + 2)
        moved = prolong(t[first:first + 4] - ends[:, n])
        full = [new[n, k] + moved[k][1:5] for k in range(4)]
        for k, (px, pz) in enumerate(PARITIES):
            stage[1 + n, pz, pl.ds(px, 32, 2)] = full[k].reshape(32, 128)
        x = jnp.concatenate([stage[1 + n, 0], stage[1 + n, 1]], -1)
        obuf[n] = pick(x, join).reshape(4, 16, 256)
        store = pltpu.make_async_copy(obuf.at[n], out_ref.at[n], out_sem.at[n])
        store.start()
        stores.append(store)
    for copy in copies:
        copy.wait_send()
    for store in stores:
        store.wait()


def solution(mesh):
    count = mesh.shape["gy"]

    def body(initial):
        f32 = jnp.float32
        tile = (8, 128)
        sends = 2 * REACH + 2 + 20 + 2
        return pl.pallas_call(
            lambda *refs: kernel(count, *refs),
            out_shape=jax.ShapeDtypeStruct((SLABS,) + initial.shape, f32),
            in_specs=[pl.BlockSpec(memory_space=pl.ANY)],
            out_specs=pl.BlockSpec(memory_space=pl.ANY),
            scratch_shapes=[
                pltpu.VMEM(initial.shape, f32),
                pltpu.VMEM((10, 4) + tile, f32),
                pltpu.VMEM((4 * REACH + OWN,) + tile, f32),
                pltpu.VMEM((18, 2) + tile, f32),
                pltpu.VMEM((14, 2) + tile, f32),
                pltpu.VMEM((10, 2) + tile, f32),
                pltpu.VMEM((6, 2) + tile, f32),
                pltpu.VMEM((4, SLABS) + tile, f32),
                pltpu.VMEM((SLABS, 4, 4) + tile, f32),
                pltpu.VMEM((1 + SLABS, 2, 64, 128), f32),
                pltpu.VMEM((SLABS,) + initial.shape, f32),
                pltpu.SemaphoreType.DMA(()),
                pltpu.SemaphoreType.DMA((SLABS,)),
                pltpu.SemaphoreType.DMA((sends,)),
                pltpu.SemaphoreType.DMA((sends,)),
            ],
            compiler_params=pltpu.CompilerParams(
                collective_id=0, has_side_effects=True, vmem_limit_bytes=32 * 1024 * 1024),
            name="pfasst",
        )(initial)

    return jax.shard_map(body, mesh=mesh, in_specs=(P("gy", "grp", None),),
                         out_specs=P(None, "gy", "grp", None), check_vma=False)
```

```python
import jax
import jax.numpy as jnp
from jax import lax
from jax.experimental import pallas as pl
from jax.experimental.pallas import tpu as pltpu
from jax.sharding import PartitionSpec as P

SLABS = 4
slab_time = 0.25
half_step = 0.125
left_weights = (5.0 / 24.0, 1.0 / 3.0, -1.0 / 24.0)
right_weights = (-1.0 / 24.0, 1.0 / 3.0, 5.0 / 24.0)
Q0 = tuple(slab_time * w for w in left_weights)
Q1 = tuple(slab_time * w for w in right_weights)

REACH = 6
OWN = 2
PARITIES = ((0, 0), (0, 1), (1, 0), (1, 1))


def lanes(x, shift):
    return pltpu.roll(x, shift % x.shape[-1], x.ndim - 1)


def rows(x, shift):
    return pltpu.roll(x, shift % x.shape[-2], x.ndim - 2)


def coarse_step(v):
    c = v[1:-1]
    beside = (v[2:] + v[:-2]) + (rows(c, 1) + rows(c, -1)) + (lanes(c, 1) + lanes(c, -1))
    return 0.03125 * beside + c * (0.9375 - 0.125 * (c * c))


def coarse_tendency(v):
    c = v[1:-1]
    beside = (v[2:] + v[:-2]) + (rows(c, 1) + rows(c, -1)) + (lanes(c, 1) + lanes(c, -1))
    return 0.25 * beside - c * (0.5 + c * c)


def fine_tendency(v):
    c = [p[1:-1] for p in v]
    out = []
    for k, (px, pz) in enumerate(PARITIES):
        x = c[2 * (1 - px) + pz]
        z = c[2 * px + 1 - pz]
        beside = (v[k][2:] + v[k][:-2]) + (x + rows(x, -1 if px else 1)) + (z + lanes(z, -1 if pz else 1))
        out.append(beside - c[k] * (5.0 + c[k] * c[k]))
    return out


def prolong(c):
    c = c * (1.0 / 64.0)
    triple = 3.0 * c
    out = []
    by_z = (triple + lanes(c, 1), triple + lanes(c, -1))
    planes = {}
    for pz in (0, 1):
        w = by_z[pz]
        triple = 3.0 * w
        planes[0, pz] = triple + rows(w, 1)
        planes[1, pz] = triple + rows(w, -1)
    for k in PARITIES:
        p = planes[k]
        triple = 3.0 * p
        odd = triple[:-1] + p[1:]
        even = triple[1:] + p[:-1]
        out.append(jnp.stack([odd, even], 1).reshape((2 * odd.shape[0],) + odd.shape[1:]))
    return out


def restrict(v):
    s = (v[0] + v[1]) + (v[2] + v[3])
    s = s.reshape((s.shape[0] // 2, 2) + s.shape[1:])
    return 0.125 * (s[:, 0] + s[:, 1])


def pick(x, table):
    high = x.astype(jnp.bfloat16)
    rest = x - high.astype(jnp.float32)
    middle = rest.astype(jnp.bfloat16)
    low = (rest - middle.astype(jnp.float32)).astype(jnp.bfloat16)
    dot = lambda p: jnp.dot(p, table, preferred_element_type=jnp.float32)
    return (dot(high) + dot(middle)) + dot(low)


def fine_slab(n, reach, old0, old1, old2, force, ends, new):
    size = 2 * (OWN + 2 * reach)
    f0 = fine_tendency(old0)
    f1 = fine_tendency(old1)
    f2 = fine_tendency(old2)
    one = [o[1:-1] + ((Q0[0] * x + Q0[1] * y) + Q0[2] * z) for o, x, y, z in zip(old0, f0, f1, f2)]
    g1 = fine_tendency(one)
    two = [o[1:-1] + (half_step * g + ((Q1[0] * x[1:-1] + (Q1[1] - half_step) * y[1:-1]) + Q1[2] * z[1:-1]))
           for o, g, x, y, z in zip(one, g1, f0, f1, f2)]
    g2 = fine_tendency(two)
    at = 2 * reach + 1
    for k in range(4):
        new[n, k] = two[k][at:at + 4]
    if reach:
        ends[n] = restrict([t[at - 2:at + 6] for t in two])
    else:
        ends[n, pl.ds(1, OWN)] = restrict([t[1:-1] for t in two])
    r0 = restrict([x[2:-2] for x in f0])
    r1 = restrict([x[1:-1] for x in g1])
    r2 = restrict(g2)
    c0 = coarse_tendency(restrict([o[1:-1] for o in old0]))
    c1 = coarse_tendency(restrict(one))
    where = pl.ds(0 if reach else 8, OWN + 2 * reach)
    force[where, 0] = (Q0[0] * r0 + Q0[1] * r1 + Q0[2] * r2) - half_step * c0
    force[where, 1] = (Q1[0] * r0 + Q1[1] * r1 + Q1[2] * r2) - half_step * c1


def kernel(count, init_ref, out_ref, raw, fine, coarse, force0, force1, force2, force3, ends, new, stage,
           in_sem, send_sem, recv_sem):
    me = lax.axis_index("gy")
    force = (force0, force1, force2, force3)

    def device(offset):
        return {"gy": lax.rem(me + (offset + count), count)}

    fetch = pltpu.make_async_copy(init_ref, raw, in_sem)
    fetch.start()
    barrier = pltpu.get_barrier_semaphore()
    for d in range(1, REACH + 1):
        for offset in (d, -d):
            pl.semaphore_signal(barrier, inc=1, device_id=device(offset))

    copies = []

    def send(src, dst, offset):
        k = len(copies)
        copy = pltpu.make_async_remote_copy(
            src_ref=src, dst_ref=dst, send_sem=send_sem.at[k], recv_sem=recv_sem.at[k], device_id=device(offset))
        copy.start()
        copies.append(copy)
        return copy

    a = lax.broadcasted_iota(jnp.int32, (256, 256), 0)
    b = lax.broadcasted_iota(jnp.int32, (256, 256), 1)
    part = (a == 2 * lax.rem(b, 128) + lax.div(b, 128)).astype(jnp.float32).astype(jnp.bfloat16)
    join = (b == 2 * lax.rem(a, 128) + lax.div(a, 128)).astype(jnp.float32).astype(jnp.bfloat16)

    fetch.wait()
    y = pick(raw[...].reshape(64, 256), part)
    stage[0, 0] = y[:, :128]
    stage[0, 1] = y[:, 128:]
    own = [stage[0, pz, pl.ds(px, 32, 2)].reshape(4, 8, 128) for px, pz in PARITIES]
    coarse[pl.ds(2 * REACH, OWN)] = restrict(own)
    for k in range(4):
        fine[pl.ds(3, 4), k] = own[k]

    pl.semaphore_wait(barrier, 2 * REACH)
    def send_rows(d):
        return [send(coarse.at[pl.ds(2 * REACH, OWN)],
                     coarse.at[pl.ds(2 * REACH - 2 * offset, OWN)], offset) for offset in (d, -d)]

    near = send_rows(1)
    near += [send(fine.at[pl.ds(4, 3)], fine.at[pl.ds(0, 3)], 1),
             send(fine.at[pl.ds(3, 3)], fine.at[pl.ds(7, 3)], -1)]
    near += send_rows(2)
    far = []
    for d in range(REACH, 2, -1):
        far += send_rows(d)

    for copy in near:
        copy.wait_recv()
    s = coarse[pl.ds(2 * REACH - 4, OWN + 8)]
    node1 = coarse_step(s)
    node2 = coarse_step(node1)
    fine_slab(0, 0, [fine[:, k] for k in range(4)], prolong(node1[1:-1]), prolong(node2), force0, ends, new)
    exchange = []
    for d in range(4, 0, -1):
        for offset in (d, -d):
            exchange.append(send(force0.at[pl.ds(8, OWN)], force0.at[pl.ds(8 - 2 * offset, OWN)], offset))
    exchange += [send(ends.at[0, 2], ends.at[0, 0], 1), send(ends.at[0, 1], ends.at[0, 3], -1)]

    for copy in far:
        copy.wait_recv()
    nodes = [coarse[...]]
    for k in range(2 * SLABS):
        nodes.append(coarse_step(nodes[-1]))
    for n in range(1, SLABS):
        fine_slab(n, 8 - 2 * n, prolong(nodes[2 * n][2:-2]), prolong(nodes[2 * n + 1][1:-1]),
                  prolong(nodes[2 * n + 2]), force[n], ends, new)

    t = coarse[2 * REACH - 9:2 * REACH + OWN + 9]
    for copy in exchange:
        copy.wait_recv()
    for n in range(SLABS):
        reach = 8 - 2 * n
        t = coarse_step(t) + force[n][:, 0]
        t = coarse_step(t) + force[n][pl.ds(1, 2 * reach), 1]
        first = reach - 2
        moved = prolong(t[first:first + 4] - ends[n])
        full = [new[n, k] + moved[k][1:5] for k in range(4)]
        for k, (px, pz) in enumerate(PARITIES):
            stage[1 + n, pz, pl.ds(px, 32, 2)] = full[k].reshape(32, 128)
        x = jnp.concatenate([stage[1 + n, 0], stage[1 + n, 1]], -1)
        out_ref[n] = pick(x, join).reshape(4, 16, 256)
    for copy in copies:
        copy.wait_send()


def solution(mesh):
    count = mesh.shape["gy"]

    def body(initial):
        f32 = jnp.float32
        tile = (8, 128)
        sends = 2 * REACH + 2 + 8 + 2
        return pl.pallas_call(
            lambda *refs: kernel(count, *refs),
            out_shape=jax.ShapeDtypeStruct((SLABS,) + initial.shape, f32),
            in_specs=[pl.BlockSpec(memory_space=pltpu.HBM)],
            out_specs=pl.BlockSpec(memory_space=pltpu.VMEM),
            scratch_shapes=[
                pltpu.VMEM(initial.shape, f32),
                pltpu.VMEM((10, 4) + tile, f32),
                pltpu.VMEM((4 * REACH + OWN,) + tile, f32),
                pltpu.VMEM((18, 2) + tile, f32),
                pltpu.VMEM((14, 2) + tile, f32),
                pltpu.VMEM((10, 2) + tile, f32),
                pltpu.VMEM((6, 2) + tile, f32),
                pltpu.VMEM((SLABS, 4) + tile, f32),
                pltpu.VMEM((SLABS, 4, 4) + tile, f32),
                pltpu.VMEM((1 + SLABS, 2, 64, 128), f32),
                pltpu.SemaphoreType.DMA(()),
                pltpu.SemaphoreType.DMA((sends,)),
                pltpu.SemaphoreType.DMA((sends,)),
            ],
            compiler_params=pltpu.CompilerParams(
                collective_id=0, has_side_effects=True, vmem_limit_bytes=32 * 1024 * 1024),
            name="pfasst",
        )(initial)

    return jax.shard_map(body, mesh=mesh, in_specs=(P("gy", "grp", None),),
                         out_specs=P(None, "gy", "grp", None), check_vma=False)
```

```python
import jax
import jax.numpy as jnp
from jax import lax
from jax.experimental import pallas as pl
from jax.experimental.pallas import tpu as pltpu
from jax.sharding import PartitionSpec as P

SLABS = 4
slab_time = 0.25
half_step = 0.125
left_weights = (5.0 / 24.0, 1.0 / 3.0, -1.0 / 24.0)
right_weights = (-1.0 / 24.0, 1.0 / 3.0, 5.0 / 24.0)
Q0 = tuple(slab_time * w for w in left_weights)
Q1 = tuple(slab_time * w for w in right_weights)

REACH = 6
OWN = 2
PARITIES = ((0, 0), (0, 1), (1, 0), (1, 1))


def lanes(x, shift):
    return pltpu.roll(x, shift % x.shape[-1], x.ndim - 1)


def rows(x, shift):
    return pltpu.roll(x, shift % x.shape[-2], x.ndim - 2)


def coarse_step(v):
    c = v[1:-1]
    beside = (v[2:] + v[:-2]) + (rows(c, 1) + rows(c, -1)) + (lanes(c, 1) + lanes(c, -1))
    return 0.03125 * beside + c * (0.9375 - 0.125 * (c * c))


def coarse_tendency(v):
    c = v[1:-1]
    beside = (v[2:] + v[:-2]) + (rows(c, 1) + rows(c, -1)) + (lanes(c, 1) + lanes(c, -1))
    return 0.25 * beside - c * (0.5 + c * c)


def fine_tendency(v):
    c = [p[1:-1] for p in v]
    out = []
    for k, (px, pz) in enumerate(PARITIES):
        x = c[2 * (1 - px) + pz]
        z = c[2 * px + 1 - pz]
        beside = (v[k][2:] + v[k][:-2]) + (x + rows(x, -1 if px else 1)) + (z + lanes(z, -1 if pz else 1))
        out.append(beside - c[k] * (5.0 + c[k] * c[k]))
    return out


def prolong(c):
    c = c * (1.0 / 64.0)
    triple = 3.0 * c
    out = []
    by_z = (triple + lanes(c, 1), triple + lanes(c, -1))
    planes = {}
    for pz in (0, 1):
        w = by_z[pz]
        triple = 3.0 * w
        planes[0, pz] = triple + rows(w, 1)
        planes[1, pz] = triple + rows(w, -1)
    for k in PARITIES:
        p = planes[k]
        triple = 3.0 * p
        odd = triple[:-1] + p[1:]
        even = triple[1:] + p[:-1]
        out.append(jnp.stack([odd, even], 1).reshape((2 * odd.shape[0],) + odd.shape[1:]))
    return out


def restrict(v):
    s = (v[0] + v[1]) + (v[2] + v[3])
    s = s.reshape((s.shape[0] // 2, 2) + s.shape[1:])
    return 0.125 * (s[:, 0] + s[:, 1])


def pick(x, table):
    high = x.astype(jnp.bfloat16)
    rest = x - high.astype(jnp.float32)
    middle = rest.astype(jnp.bfloat16)
    low = (rest - middle.astype(jnp.float32)).astype(jnp.bfloat16)
    dot = lambda p: jnp.dot(p, table, preferred_element_type=jnp.float32)
    return (dot(high) + dot(middle)) + dot(low)


def fine_slab(n, reach, old0, old1, old2, ends, new):
    size = 2 * (OWN + 2 * reach)
    f0 = fine_tendency(old0)
    f1 = fine_tendency(old1)
    f2 = fine_tendency(old2)
    one = [o[1:-1] + ((Q0[0] * x + Q0[1] * y) + Q0[2] * z) for o, x, y, z in zip(old0, f0, f1, f2)]
    g1 = fine_tendency(one)
    two = [o[1:-1] + (half_step * g + ((Q1[0] * x[1:-1] + (Q1[1] - half_step) * y[1:-1]) + Q1[2] * z[1:-1]))
           for o, g, x, y, z in zip(one, g1, f0, f1, f2)]
    g2 = fine_tendency(two)
    at = 2 * reach + 1
    for k in range(4):
        new[n, k] = two[k][at:at + 4]
    if reach:
        ends[n] = restrict([t[at - 2:at + 6] for t in two])
    else:
        ends[n, pl.ds(1, OWN)] = restrict([t[1:-1] for t in two])
    r0 = restrict([x[2:-2] for x in f0])
    r1 = restrict([x[1:-1] for x in g1])
    r2 = restrict(g2)
    c0 = coarse_tendency(restrict([o[1:-1] for o in old0]))
    c1 = coarse_tendency(restrict(one))
    return ((Q0[0] * r0 + Q0[1] * r1 + Q0[2] * r2) - half_step * c0,
            (Q1[0] * r0 + Q1[1] * r1 + Q1[2] * r2) - half_step * c1)


def table(axis):
    wide = lax.broadcasted_iota(jnp.int32, (256, 256), axis)
    split = lax.broadcasted_iota(jnp.int32, (256, 256), 1 - axis)
    return (wide == ((split & 127) << 1) + (split >> 7)).astype(jnp.float32).astype(jnp.bfloat16)


def kernel(count, init_ref, out_ref, fine, coarse, force0, force1, force2, force3, ends, new, stage,
           send_sem, recv_sem):
    me = lax.axis_index("gy")
    force = (force0, force1, force2, force3)

    def device(offset):
        return {"gy": lax.rem(me + (offset + count), count)}

    barrier = pltpu.get_barrier_semaphore()
    for d in range(1, REACH + 1):
        for offset in (d, -d):
            pl.semaphore_signal(barrier, inc=1, device_id=device(offset))

    copies = []

    def send(src, dst, offset):
        k = len(copies)
        copy = pltpu.make_async_remote_copy(
            src_ref=src, dst_ref=dst, send_sem=send_sem.at[k], recv_sem=recv_sem.at[k], device_id=device(offset))
        copy.start()
        copies.append(copy)
        return copy

    y = pick(init_ref[...].reshape(64, 256), table(0))
    stage[0, 0] = y[:, :128]
    stage[0, 1] = y[:, 128:]
    own = [stage[0, pz, pl.ds(px, 32, 2)].reshape(4, 8, 128) for px, pz in PARITIES]
    coarse[pl.ds(2 * REACH, OWN)] = restrict(own)
    for k in range(4):
        fine[pl.ds(3, 4), k] = own[k]

    pl.semaphore_wait(barrier, 2 * REACH)
    def send_rows(d):
        return [send(coarse.at[pl.ds(2 * REACH, OWN)],
                     coarse.at[pl.ds(2 * REACH - 2 * offset, OWN)], offset) for offset in (d, -d)]

    near = send_rows(1)
    near += [send(fine.at[pl.ds(4, 3)], fine.at[pl.ds(0, 3)], 1),
             send(fine.at[pl.ds(3, 3)], fine.at[pl.ds(7, 3)], -1)]
    near += send_rows(2)
    far = []
    for d in range(3, REACH + 1):
        far += send_rows(d)

    join = table(1)
    for copy in near:
        copy.wait_recv()
    s = coarse[pl.ds(2 * REACH - 4, OWN + 8)]
    node1 = coarse_step(s)
    node2 = coarse_step(node1)
    start, middle = fine_slab(0, 0, [fine[:, k] for k in range(4)], prolong(node1[1:-1]), prolong(node2), ends, new)
    force0[4, 0] = middle[0]
    force0[4, 1:3] = start
    force0[4, 3] = middle[1]
    exchange = []
    for d in range(1, 5):
        for offset in (d, -d):
            part = pl.ds(0, 4) if d < 4 else pl.ds(1 if offset > 0 else 0, 3)
            exchange.append(send(force0.at[4, part], force0.at[4 - offset, part], offset))
    exchange += [send(ends.at[0, 2], ends.at[0, 0], 1), send(ends.at[0, 1], ends.at[0, 3], -1)]

    for copy in far:
        copy.wait_recv()
    nodes = [coarse[...]]
    for k in range(2 * SLABS):
        nodes.append(coarse_step(nodes[-1]))
    for n in range(1, SLABS):
        start, middle = fine_slab(n, 8 - 2 * n, prolong(nodes[2 * n][2:-2]), prolong(nodes[2 * n + 1][1:-1]),
                                  prolong(nodes[2 * n + 2]), ends, new)
        force[n][:, 0] = start
        force[n][:, 1] = middle

    t = coarse[2 * REACH - 9:2 * REACH + OWN + 9]
    step = coarse_step(t)
    for copy in exchange:
        copy.wait_recv()
    for n in range(SLABS):
        reach = 8 - 2 * n
        if n == 0:
            start = force0[:, 1:3].reshape(18, 8, 128)
            middle = jnp.stack([force0[0:8, 3], force0[1:9, 0]], 1).reshape(16, 8, 128)
        else:
            start, middle = force[n][:, 0], force[n][pl.ds(1, 2 * reach), 1]
        t = (step if n == 0 else coarse_step(t)) + start
        t = coarse_step(t) + middle
        first = reach - 2
        moved = prolong(t[first:first + 4] - ends[n])
        full = [new[n, k] + moved[k][1:5] for k in range(4)]
        for k, (px, pz) in enumerate(PARITIES):
            stage[1 + n, pz, pl.ds(px, 32, 2)] = full[k].reshape(32, 128)
        x = jnp.concatenate([stage[1 + n, 0], stage[1 + n, 1]], -1)
        out_ref[n] = pick(x, join).reshape(4, 16, 256)
    for copy in copies:
        copy.wait_send()


def solution(mesh):
    count = mesh.shape["gy"]

    def body(initial):
        f32 = jnp.float32
        tile = (8, 128)
        sends = 2 * REACH + 2 + 8 + 2
        return pl.pallas_call(
            lambda *refs: kernel(count, *refs),
            out_shape=jax.ShapeDtypeStruct((SLABS,) + initial.shape, f32),
            in_specs=[pl.BlockSpec(memory_space=pltpu.VMEM)],
            out_specs=pl.BlockSpec(memory_space=pltpu.VMEM),
            scratch_shapes=[
                pltpu.VMEM((10, 4) + tile, f32),
                pltpu.VMEM((4 * REACH + OWN,) + tile, f32),
                pltpu.VMEM((9, 4) + tile, f32),
                pltpu.VMEM((14, 2) + tile, f32),
                pltpu.VMEM((10, 2) + tile, f32),
                pltpu.VMEM((6, 2) + tile, f32),
                pltpu.VMEM((SLABS, 4) + tile, f32),
                pltpu.VMEM((SLABS, 4, 4) + tile, f32),
                pltpu.VMEM((1 + SLABS, 2, 64, 128), f32),
                pltpu.SemaphoreType.DMA((sends,)),
                pltpu.SemaphoreType.DMA((sends,)),
            ],
            compiler_params=pltpu.CompilerParams(
                collective_id=0, has_side_effects=True, vmem_limit_bytes=32 * 1024 * 1024),
            name="pfasst",
        )(initial)

    return jax.shard_map(body, mesh=mesh, in_specs=(P("gy", "grp", None),),
                         out_specs=P(None, "gy", "grp", None), check_vma=False)
```

```python
import jax
import jax.numpy as jnp
from jax import lax
from jax.experimental import pallas as pl
from jax.experimental.pallas import tpu as pltpu
from jax.sharding import PartitionSpec as P

SLABS = 4
slab_time = 0.25
half_step = 0.125
left_weights = (5.0 / 24.0, 1.0 / 3.0, -1.0 / 24.0)
right_weights = (-1.0 / 24.0, 1.0 / 3.0, 5.0 / 24.0)
Q0 = tuple(slab_time * w for w in left_weights)
Q1 = tuple(slab_time * w for w in right_weights)

REACH = 6
OWN = 2
PARITIES = ((0, 0), (0, 1), (1, 0), (1, 1))


def lanes(x, shift):
    return pltpu.roll(x, shift % x.shape[-1], x.ndim - 1)


def rows(x, shift):
    return pltpu.roll(x, shift % x.shape[-2], x.ndim - 2)


def coarse_step(v):
    c = v[1:-1]
    beside = (v[2:] + v[:-2]) + (rows(c, 1) + rows(c, -1)) + (lanes(c, 1) + lanes(c, -1))
    return 0.03125 * beside + c * (0.9375 - 0.125 * (c * c))


def coarse_tendency(v):
    c = v[1:-1]
    beside = (v[2:] + v[:-2]) + (rows(c, 1) + rows(c, -1)) + (lanes(c, 1) + lanes(c, -1))
    return 0.25 * beside - c * (0.5 + c * c)


def fine_tendency(v):
    c = [p[1:-1] for p in v]
    out = []
    for k, (px, pz) in enumerate(PARITIES):
        x = c[2 * (1 - px) + pz]
        z = c[2 * px + 1 - pz]
        beside = (v[k][2:] + v[k][:-2]) + (x + rows(x, -1 if px else 1)) + (z + lanes(z, -1 if pz else 1))
        out.append(beside - c[k] * (5.0 + c[k] * c[k]))
    return out


def prolong(c):
    c = c * (1.0 / 64.0)
    triple = 3.0 * c
    out = []
    by_z = (triple + lanes(c, 1), triple + lanes(c, -1))
    planes = {}
    for pz in (0, 1):
        w = by_z[pz]
        triple = 3.0 * w
        planes[0, pz] = triple + rows(w, 1)
        planes[1, pz] = triple + rows(w, -1)
    for k in PARITIES:
        p = planes[k]
        triple = 3.0 * p
        odd = triple[:-1] + p[1:]
        even = triple[1:] + p[:-1]
        out.append(jnp.stack([odd, even], 1).reshape((2 * odd.shape[0],) + odd.shape[1:]))
    return out


def restrict(v):
    s = (v[0] + v[1]) + (v[2] + v[3])
    s = s.reshape((s.shape[0] // 2, 2) + s.shape[1:])
    return 0.125 * (s[:, 0] + s[:, 1])


def pick(x, table):
    high = x.astype(jnp.bfloat16)
    rest = x - high.astype(jnp.float32)
    middle = rest.astype(jnp.bfloat16)
    low = (rest - middle.astype(jnp.float32)).astype(jnp.bfloat16)
    dot = lambda p: jnp.dot(p, table, preferred_element_type=jnp.float32)
    return (dot(high) + dot(middle)) + dot(low)


def fine_slab(n, reach, old0, old1, old2, ends, new):
    size = 2 * (OWN + 2 * reach)
    f0 = fine_tendency(old0)
    f1 = fine_tendency(old1)
    f2 = fine_tendency(old2)
    one = [o[1:-1] + ((Q0[0] * x + Q0[1] * y) + Q0[2] * z) for o, x, y, z in zip(old0, f0, f1, f2)]
    g1 = fine_tendency(one)
    two = [o[1:-1] + (half_step * g + ((Q1[0] * x[1:-1] + (Q1[1] - half_step) * y[1:-1]) + Q1[2] * z[1:-1]))
           for o, g, x, y, z in zip(one, g1, f0, f1, f2)]
    g2 = fine_tendency(two)
    at = 2 * reach + 1
    for k in range(4):
        new[n, k] = two[k][at:at + 4]
    if reach:
        ends[n] = restrict([t[at - 2:at + 6] for t in two])
    else:
        ends[n, pl.ds(1, OWN)] = restrict([t[1:-1] for t in two])
    r0 = restrict([x[2:-2] for x in f0])
    r1 = restrict([x[1:-1] for x in g1])
    r2 = restrict(g2)
    c0 = coarse_tendency(restrict([o[1:-1] for o in old0]))
    c1 = coarse_tendency(restrict(one))
    return ((Q0[0] * r0 + Q0[1] * r1 + Q0[2] * r2) - half_step * c0,
            (Q1[0] * r0 + Q1[1] * r1 + Q1[2] * r2) - half_step * c1)


def table(axis):
    wide = lax.broadcasted_iota(jnp.int32, (256, 256), axis)
    split = lax.broadcasted_iota(jnp.int32, (256, 256), 1 - axis)
    return (wide == ((split & 127) << 1) + (split >> 7)).astype(jnp.float32).astype(jnp.bfloat16)


def kernel(count, init_ref, out_ref, fine, coarse, force0, force1, force2, force3, ends, new, stage,
           send_sem, recv_sem):
    me = lax.axis_index("gy")
    force = (force0, force1, force2, force3)

    def device(offset):
        return {"gy": lax.rem(me + (offset + count), count)}

    barrier = pltpu.get_barrier_semaphore()
    for d in range(REACH, 0, -1):
        for offset in (d, -d):
            pl.semaphore_signal(barrier, inc=1, device_id=device(offset))

    copies = []

    def send(src, dst, offset):
        k = len(copies)
        copy = pltpu.make_async_remote_copy(
            src_ref=src, dst_ref=dst, send_sem=send_sem.at[k], recv_sem=recv_sem.at[k], device_id=device(offset))
        copy.start()
        copies.append(copy)
        return copy

    y = pick(init_ref[...].reshape(64, 256), table(0))
    stage[0, 0] = y[:, :128]
    stage[0, 1] = y[:, 128:]
    own = [stage[0, pz, pl.ds(px, 32, 2)].reshape(4, 8, 128) for px, pz in PARITIES]
    coarse[pl.ds(2 * REACH, OWN)] = restrict(own)
    for k in range(4):
        fine[pl.ds(3, 4), k] = own[k]

    pl.semaphore_wait(barrier, 2 * REACH)
    def send_rows(d):
        return [send(coarse.at[pl.ds(2 * REACH, OWN)],
                     coarse.at[pl.ds(2 * REACH - 2 * offset, OWN)], offset) for offset in (d, -d)]

    near = send_rows(1)
    near += [send(fine.at[pl.ds(4, 3)], fine.at[pl.ds(0, 3)], 1),
             send(fine.at[pl.ds(3, 3)], fine.at[pl.ds(7, 3)], -1)]
    near += send_rows(2)
    far = []
    for d in range(3, REACH + 1):
        far += send_rows(d)

    join = table(1)
    for copy in near:
        copy.wait_recv()
    s = coarse[pl.ds(2 * REACH - 4, OWN + 8)]
    node1 = coarse_step(s)
    node2 = coarse_step(node1)
    start, middle = fine_slab(0, 0, [fine[:, k] for k in range(4)], prolong(node1[1:-1]), prolong(node2), ends, new)
    force0[4, 0] = middle[0]
    force0[4, 1:3] = start
    force0[4, 3] = middle[1]
    exchange = []
    for d in range(1, 5):
        for offset in (d, -d):
            part = pl.ds(0, 4) if d < 4 else pl.ds(1 if offset > 0 else 0, 3)
            exchange.append(send(force0.at[4, part], force0.at[4 - offset, part], offset))
    exchange += [send(ends.at[0, 2], ends.at[0, 0], 1), send(ends.at[0, 1], ends.at[0, 3], -1)]

    for copy in far:
        copy.wait_recv()
    nodes = [coarse[...]]
    for k in range(2 * SLABS):
        nodes.append(coarse_step(nodes[-1]))
    for n in range(1, SLABS):
        start, middle = fine_slab(n, 8 - 2 * n, prolong(nodes[2 * n][2:-2]), prolong(nodes[2 * n + 1][1:-1]),
                                  prolong(nodes[2 * n + 2]), ends, new)
        force[n][:, 0] = start
        force[n][:, 1] = middle

    t = coarse[2 * REACH - 9:2 * REACH + OWN + 9]
    step = coarse_step(t)
    for copy in exchange:
        copy.wait_recv()
    for n in range(SLABS):
        reach = 8 - 2 * n
        if n == 0:
            start = force0[:, 1:3].reshape(18, 8, 128)
            middle = jnp.stack([force0[0:8, 3], force0[1:9, 0]], 1).reshape(16, 8, 128)
        else:
            start, middle = force[n][:, 0], force[n][pl.ds(1, 2 * reach), 1]
        t = (step if n == 0 else coarse_step(t)) + start
        t = coarse_step(t) + middle
        first = reach - 2
        moved = prolong(t[first:first + 4] - ends[n])
        full = [new[n, k] + moved[k][1:5] for k in range(4)]
        for k, (px, pz) in enumerate(PARITIES):
            stage[1 + n, pz, pl.ds(px, 32, 2)] = full[k].reshape(32, 128)
        x = jnp.concatenate([stage[1 + n, 0], stage[1 + n, 1]], -1)
        out_ref[n] = pick(x, join).reshape(4, 16, 256)
    for copy in copies:
        copy.wait_send()


def solution(mesh):
    count = mesh.shape["gy"]

    def body(initial):
        f32 = jnp.float32
        tile = (8, 128)
        sends = 2 * REACH + 2 + 8 + 2
        return pl.pallas_call(
            lambda *refs: kernel(count, *refs),
            out_shape=jax.ShapeDtypeStruct((SLABS,) + initial.shape, f32),
            in_specs=[pl.BlockSpec(memory_space=pltpu.VMEM)],
            out_specs=pl.BlockSpec(memory_space=pltpu.VMEM),
            scratch_shapes=[
                pltpu.VMEM((10, 4) + tile, f32),
                pltpu.VMEM((4 * REACH + OWN,) + tile, f32),
                pltpu.VMEM((9, 4) + tile, f32),
                pltpu.VMEM((14, 2) + tile, f32),
                pltpu.VMEM((10, 2) + tile, f32),
                pltpu.VMEM((6, 2) + tile, f32),
                pltpu.VMEM((SLABS, 4) + tile, f32),
                pltpu.VMEM((SLABS, 4, 4) + tile, f32),
                pltpu.VMEM((1 + SLABS, 2, 64, 128), f32),
                pltpu.SemaphoreType.DMA((sends,)),
                pltpu.SemaphoreType.DMA((sends,)),
            ],
            compiler_params=pltpu.CompilerParams(
                collective_id=0, has_side_effects=True, vmem_limit_bytes=32 * 1024 * 1024),
            name="pfasst",
        )(initial)

    return jax.shard_map(body, mesh=mesh, in_specs=(P("gy", "grp", None),),
                         out_specs=P(None, "gy", "grp", None), check_vma=False)
```
